32 devices in a mesh: prow: 8 (over z, x), pcol: 4 (over y, core).
Axes of the slice: x: 2, y: 2, z: 4, core: 2. Of those that a mesh axis runs over, the one named last changes fastest.
Arguments:
- right_hand_blocks: float32 [8, 4, 512, 256], P('prow'), may hold values from -6 to 6
- diag_inverse: bfloat16 [8, 4, 512, 512], P('prow'), as said below
- lower_blocks: bfloat16 [8, 4, 3, 5, 512, 512], P('prow', 'pcol'), may hold values from -0.0625 to 0.0625
- block_source: int32 [8, 4, 3, 5], P('prow', 'pcol'), may hold values from 0 to 1, as said below
- target_level_per_slot: int32 [8, 4, 3, 5], P('prow', 'pcol'), may hold values from 1 to 4, as said below
Outputs:
- solved: bfloat16 [8, 4, 512, 256], P('prow')
The draws below stay inside these ranges and needn't reach their ends.
Inputs may be any that keep to these rules, and one draw needn't show every extreme that they name: `target_level_per_slot`: block (source k, target level t) appears at most once among the slots of one device and one source level l; every target level exceeds l; the filled slots come first, and there are min(5, 2 * (3 - l)) of them. `block_source`: an empty slot has source 0. `diag_inverse`: lower triangular, diagonal between 0.5 and 1.5.
All inputs are finite; a program needn't handle non-finite values.
Results may differ from the reference program's by a relative error of at most 0.0075.
Values may be sent and summed in bfloat16 or wider, within the bound.
A program may use at most 128 MiB of HBM per device.

```python
import math
import jax
import jax.numpy as jnp
from jax import lax

W = 512
RHS = 256
LEVELS = 4
NBL = 5
N_PROW = 8
N_PCOL = 4


def draw_diag_inverse(key, part):
    full_shape = (N_PROW, LEVELS, W, W)
    lower_mask = jnp.tril(jnp.ones((W, W), jnp.float32), -1)
    broadcast_update = jax.random.normal(jax.random.fold_in(key, 1), full_shape, jnp.float32) * 0.6
    diagonal = jax.random.uniform(jax.random.fold_in(key, 2), full_shape[:3], jnp.float32, 0.5, 1.5)
    whole = broadcast_update * lower_mask / math.sqrt(W) + diagonal[..., None] * jnp.eye(W, dtype=jnp.float32)
    return whole.astype(jnp.bfloat16)


def structure_lists(key):
    per_col = N_PROW // N_PCOL
    most_pairs = per_col * (LEVELS - 1)
    entry_count = N_PROW * N_PCOL * (LEVELS - 1)
    entry_keys = jax.random.split(jax.random.fold_in(key, 11), entry_count)
    tree_levels = jnp.tile(jnp.arange(LEVELS - 1, dtype=jnp.int32), N_PROW * N_PCOL)

    def one_list(entry_key, tree_level):
        priority = jax.random.permutation(entry_key, most_pairs).astype(jnp.int32)
        pair_index = jnp.arange(most_pairs, dtype=jnp.int32)
        pair_limit = per_col * (LEVELS - 1 - tree_level)
        sort_key = jnp.where(pair_index < pair_limit, priority, most_pairs + pair_index)
        selected_slots = jnp.argsort(sort_key, stable=True)[:NBL].astype(jnp.int32)
        filled = jnp.arange(NBL, dtype=jnp.int32) < pair_limit
        sources = jnp.where(filled, selected_slots % per_col, 0).astype(jnp.int32)
        targets = jnp.where(filled, tree_level + 1 + selected_slots // per_col, LEVELS).astype(jnp.int32)
        return (sources, targets)
    sources, targets = jax.vmap(one_list)(entry_keys, tree_levels)
    return (sources.reshape(N_PROW, N_PCOL, LEVELS - 1, NBL), targets.reshape(N_PROW, N_PCOL, LEVELS - 1, NBL))


def draw_block_source(key, part):
    return structure_lists(key)[0]


def draw_target_level_per_slot(key, part):
    return structure_lists(key)[1]


def steps_of(own_key, extent, cuts, smallest, top_value):
    def one(axis_at, parts):
        draws = jax.random.uniform(jax.random.fold_in(jax.random.fold_in(own_key, 6), axis_at), (parts,), jnp.float32, smallest / len(cuts), top_value / len(cuts))
        return jnp.repeat(jnp.exp(draws), extent[axis_at] // parts).reshape((-1,) + (1,) * (len(extent) - axis_at - 1))

    factor_of = one(*cuts[0])
    for cut in cuts[1:]:
        factor_of = factor_of * one(*cut)
    return factor_of


def noise(stream_key, extent, deviation, bound, cuts=(), held_as=jnp.bfloat16):
    array = deviation * jax.random.normal(stream_key, extent, jnp.float32)
    if cuts:
        array = array * steps_of(stream_key, extent, cuts, -0.22, 0.18)
    return jnp.clip(array, -bound, bound).astype(held_as)


def setup_inputs(seed: int = 0) -> dict:
    seeds = jax.random.split(jax.random.key(seed), 6)
    return {
        "right_hand_blocks": noise(seeds[0], (N_PROW, LEVELS, W, RHS), 1.0, 6.0, ((0, 8),), jnp.float32),
        "diag_inverse": draw_diag_inverse(jax.random.fold_in(seeds[5], 71), 0),
        "lower_blocks": noise(seeds[2], (N_PROW, N_PCOL, LEVELS - 1, NBL, W, W), (4 * W * N_PCOL) ** -0.5, 0.0625, ((0, 8), (1, 4))),
        "block_source": draw_block_source(jax.random.fold_in(seeds[5], 71), 0),
        "target_level_per_slot": draw_target_level_per_slot(jax.random.fold_in(seeds[5], 71), 0),
    }


def reference(right_hand_blocks, diag_inverse, lower_blocks, block_source, target_level_per_slot):
    row_count = right_hand_blocks.shape[0]
    levels = right_hand_blocks.shape[1]
    per_col = row_count // N_PCOL
    partial_value = jnp.zeros((levels, row_count, W, RHS), jnp.float32)
    outputs = []
    for tree_level in range(levels):
        rhs_block = (right_hand_blocks[:, tree_level] - partial_value[tree_level]).astype(jnp.bfloat16)
        solved = jnp.einsum("sij,sjr->sir", diag_inverse[:, tree_level].astype(jnp.float32),
                            rhs_block.astype(jnp.float32)).astype(jnp.bfloat16)
        outputs.append(solved)
        if tree_level < levels - 1:
            by_col = solved.reshape(per_col, N_PCOL, W, RHS).transpose(1, 0, 2, 3)

            def single_row_entry(row_args):
                blocks, sources, targets = row_args
                picked = by_col[jnp.arange(N_PCOL, dtype=jnp.int32)[:, None], sources]
                block_products = jnp.einsum("cbij,cbjr->cbir", blocks.astype(jnp.float32), picked.astype(jnp.float32))
                indicator_matrix = (targets[None, :, :] == jnp.arange(levels, dtype=jnp.int32)[:, None, None]).astype(jnp.float32)
                return jnp.einsum("wvx,vxsg->wsg", indicator_matrix, block_products, precision=lax.Precision.HIGHEST)

            row_contributions = lax.map(single_row_entry, (lower_blocks[:, :, tree_level], block_source[:, :, tree_level],
                                          target_level_per_slot[:, :, tree_level]))
            partial_value = partial_value + row_contributions.transpose(1, 0, 2, 3)
    return jnp.stack(outputs, axis=1)
```

```python
import functools

import jax
import jax.numpy as jnp
from jax import lax
from jax.experimental import pallas as pl
from jax.experimental.pallas import tpu as pltpu
from jax.sharding import PartitionSpec as P

MESH = pl.DeviceIdType.MESH
F32 = jnp.float32
BF16 = jnp.bfloat16


def kernel(dims, *refs):
    rows, cols, levels, width, half, slots = dims
    nx, ny = cols // 2, cols // 2
    nz = rows // nx
    per_col = rows // cols
    step_z = cols // nx
    (rhs_hbm, diag_hbm, low_hbm, src_ref, tgt_ref, out_hbm) = refs[:6]
    (rhs0, rhsh, diag, block, acc, mine, pair_out, pair_in, cross) = refs[6:15]
    low = refs[15:15 + levels - 1]
    (rhs_sem, diag_sem, low_sem, out_sem, b_send, b_recv, p_send, p_recv,
     y_send, y_recv, m_send, m_recv) = refs[15 + levels - 1:]

    r = lax.axis_index("prow")
    c = lax.axis_index("pcol")
    z, x = r // nx, lax.rem(r, nx)
    y, core = c // 2, lax.rem(c, 2)
    other = 1 - core
    spine_x = lax.rem(c, nx)
    is_spine = x == spine_x
    first_z = c // nx
    sibling = (r, y * 2 + other)

    def across(j):
        return (r, lax.rem(y + j, ny) * 2 + core)

    loads_rhs = [pltpu.make_async_copy(rhs_hbm.at[0, 0], rhs0, rhs_sem.at[0])]
    col_half = pl.ds(pl.multiple_of(core * half, half), half)
    for l in range(1, levels):
        loads_rhs.append(pltpu.make_async_copy(
            rhs_hbm.at[0, l, :, col_half], rhsh.at[l - 1], rhs_sem.at[l]))
    loads_diag = [pltpu.make_async_copy(diag_hbm.at[0, l], diag.at[l], diag_sem.at[l])
                  for l in range(levels)]
    loads_low = [pltpu.make_async_copy(
        low_hbm.at[0, 0, l, pl.ds(0, low[l].shape[0])], low[l], low_sem.at[l])
        for l in range(levels - 1)]
    for l in range(levels):
        loads_rhs[l].start()
        loads_diag[l].start()
        if l < levels - 1:
            loads_low[l].start()

    barrier = pltpu.get_barrier_semaphore()

    def greet(device):
        pl.semaphore_signal(barrier, inc=1, device_id=device, device_id_type=MESH)

    greet(sibling)
    for j in range(1, ny):
        greet(across(j))

    @pl.when(is_spine)
    def _():
        for j in range(1, nx):
            greet((z * nx + lax.rem(x + j, nx), c))

        @pl.when(z > 0)
        def _():
            greet((r - nx, c))

        @pl.when(z < nz - 1)
        def _():
            greet((r + nx, c))

    @pl.when(jnp.logical_not(is_spine))
    def _():
        greet((z * nx + spine_x, c))
    ends = jnp.where(z > 0, 1, 0) + jnp.where(z < nz - 1, 1, 0)
    pl.semaphore_wait(barrier, ny + jnp.where(is_spine, nx - 1 + ends, 1))

    def b_copy(l, k, h, lane, device):
        return pltpu.make_async_remote_copy(
            src_ref=block.at[l, k, h], dst_ref=block.at[l, k, h],
            send_sem=b_send.at[l, k, h, lane], recv_sem=b_recv.at[l, k, h],
            device_id=device, device_id_type=MESH)

    def on_routes(l, k, h, act):
        origin = first_z + k * step_z

        @pl.when(is_spine)
        def _():
            @pl.when(jnp.logical_and(z >= origin, z < nz - 1))
            def _():
                act(b_copy(l, k, h, 0, (r + nx, c)))

            @pl.when(jnp.logical_and(z <= origin, z > 0))
            def _():
                act(b_copy(l, k, h, 1, (r - nx, c)))
            for j in range(1, nx):
                act(b_copy(l, k, h, 1 + j, (z * nx + lax.rem(x + j, nx), c)))

    def is_root(k):
        return jnp.logical_and(is_spine, z == first_z + k * step_z)

    def publish(l, h, value):
        for k in range(per_col):
            @pl.when(is_root(k))
            def _():
                block[l, k, h] = value
                on_routes(l, k, h, lambda copy: copy.start())

    def p_copy(l):
        return pltpu.make_async_remote_copy(
            src_ref=pair_out.at[l], dst_ref=pair_in.at[l], send_sem=p_send.at[l],
            recv_sem=p_recv.at[l], device_id=sibling, device_id_type=MESH)

    def y_copy(l, j):
        return pltpu.make_async_remote_copy(
            src_ref=cross.at[l, y], dst_ref=cross.at[l, y], send_sem=y_send.at[l, j - 1],
            recv_sem=y_recv.at[l, j - 1], device_id=across(j), device_id_type=MESH)

    def m_copy(l):
        return pltpu.make_async_remote_copy(
            src_ref=mine.at[l, core], dst_ref=mine.at[l, core], send_sem=m_send.at[l],
            recv_sem=m_recv.at[l], device_id=sibling, device_id_type=MESH)

    def put_out(l):
        return [pltpu.make_async_copy(
            mine.at[l, h], out_hbm.at[0, l, :, pl.ds(h * half, half)], out_sem.at[l, h])
            for h in range(2)]

    def pair_slot(l, k, t):
        slot, there = jnp.int32(0), jnp.int32(0)
        for b in range(low[l].shape[0]):
            hit = jnp.where(
                jnp.logical_and(src_ref[0, 0, l, b] == k, tgt_ref[0, 0, l, b] == t), 1, 0)
            slot, there = slot + b * hit, there + hit
        return slot, there

    def product(l, k, t, right):
        slot, there = pair_slot(l, k, t)
        value = jnp.dot(low[l][slot], right, preferred_element_type=F32)
        if per_col * (levels - 1 - l) > slots:
            value = jnp.where(there > 0, value, 0.0)
        return value

    loads_rhs[0].wait()
    loads_diag[0].wait()
    solved = jnp.dot(diag[0], rhs0[...].astype(BF16), preferred_element_type=F32).astype(BF16)
    for h in range(2):
        publish(0, h, solved[:, h * half:(h + 1) * half])
    for h in range(2):
        mine[0, h] = solved[:, h * half:(h + 1) * half]
    for copy in put_out(0):
        copy.start()

    low_z = z < nz // 2
    for l in range(levels - 1):
        t = l + 1
        for i in range(per_col):
            k = jnp.where(low_z, i, per_col - 1 - i)
            for h in (core, other):
                @pl.when(jnp.logical_not(is_root(k)))
                def _():
                    b_copy(l, k, h, 0, sibling).wait_recv()
                    on_routes(l, k, h, lambda copy: copy.start())
        loads_low[l].wait()

        def next_partial(h):
            total = None
            for k in range(per_col):
                value = product(l, k, t, block[l, k, h])
                total = value if total is None else total + value
            if l > 0:
                total = total + acc[t - 1, h]
            return total

        pair_out[l] = next_partial(other).astype(BF16)
        p_copy(l).start()
        own = next_partial(core)
        p_copy(l).wait_recv()
        cross[l, y] = (own + pair_in[l].astype(F32)).astype(BF16)
        for j in range(1, ny):
            y_copy(l, j).start()

        for later in range(l + 2, levels):
            total = None
            for k in range(per_col):
                right = jnp.concatenate([block[l, k, 0], block[l, k, 1]], axis=1)
                value = product(l, k, later, right)
                total = value if total is None else total + value
            for h in range(2):
                part = total[:, h * half:(h + 1) * half]
                acc[later - 1, h] = part if l == 0 else acc[later - 1, h] + part

        loads_rhs[t].wait()
        loads_diag[t].wait()
        for j in range(1, ny):
            y_copy(l, j).wait_recv()
        summed = cross[l, 0].astype(F32)
        for j in range(1, ny):
            summed = summed + cross[l, j].astype(F32)
        reduced = (rhsh[t - 1] - summed).astype(BF16)
        solved = jnp.dot(diag[t], reduced, preferred_element_type=F32).astype(BF16)
        mine[t, core] = solved
        m_copy(t).start()
        if t < levels - 1:
            publish(t, core, solved)
        m_copy(t).wait_recv()
        if t < levels - 1:
            publish(t, other, mine[t, other])
        for copy in put_out(t):
            copy.start()

    for l in range(levels):
        for copy in put_out(l):
            copy.wait()
        if l > 0:
            m_copy(l).wait_send()
        if l < levels - 1:
            p_copy(l).wait_send()
            for j in range(1, ny):
                y_copy(l, j).wait_send()
            for k in range(per_col):
                for h in range(2):
                    on_routes(l, k, h, lambda copy: copy.wait_send())


def on_device(mesh_sizes, right_hand_blocks, diag_inverse, lower_blocks, block_source,
              target_level_per_slot):
    rows, cols = mesh_sizes
    _, levels, width, rhs_cols = right_hand_blocks.shape
    slots = lower_blocks.shape[3]
    half = rhs_cols // 2
    per_col = rows // cols
    nx, ny = cols // 2, cols // 2
    filled = [min(slots, per_col * (levels - 1 - l)) for l in range(levels - 1)]
    dma = pltpu.SemaphoreType.DMA
    steps = levels - 1
    piece = (width, half)
    products = sum(filled) + levels
    return pl.pallas_call(
        functools.partial(kernel, (rows, cols, levels, width, half, slots)),
        out_shape=jax.ShapeDtypeStruct((1, levels, width, rhs_cols), BF16),
        in_specs=[pl.BlockSpec(memory_space=pl.ANY)] * 3
        + [pl.BlockSpec(memory_space=pltpu.SMEM)] * 2,
        out_specs=pl.BlockSpec(memory_space=pl.ANY),
        scratch_shapes=[
            pltpu.VMEM((width, rhs_cols), F32),
            pltpu.VMEM((steps,) + piece, F32),
            pltpu.VMEM((levels, width, width), BF16),
            pltpu.VMEM((steps, per_col, 2) + piece, BF16),
            pltpu.VMEM((steps, 2) + piece, F32),
            pltpu.VMEM((levels, 2) + piece, BF16),
            pltpu.VMEM((steps,) + piece, BF16),
            pltpu.VMEM((steps,) + piece, BF16),
            pltpu.VMEM((steps, ny) + piece, BF16),
        ]
        + [pltpu.VMEM((n, width, width), BF16) for n in filled]
        + [
            dma((levels,)), dma((levels,)), dma((steps,)), dma((levels, 2)),
            dma((steps, per_col, 2, nx + 1)), dma((steps, per_col, 2)),
            dma((steps,)), dma((steps,)),
            dma((steps, ny - 1)), dma((steps, ny - 1)),
            dma((levels,)), dma((levels,)),
        ],
        compiler_params=pltpu.CompilerParams(
            collective_id=0, has_side_effects=True, vmem_limit_bytes=56 * 2**20),
        cost_estimate=pl.CostEstimate(
            flops=2 * products * width * width * rhs_cols,
            bytes_accessed=products * width * width * 2 + levels * width * rhs_cols * 6,
            transcendentals=0),
    )(right_hand_blocks, diag_inverse, lower_blocks, block_source, target_level_per_slot)


def solution(mesh):
    placed = (
        P("prow", None, None, None),
        P("prow", None, None, None),
        P("prow", "pcol", None, None, None, None),
        P("prow", "pcol", None, None),
        P("prow", "pcol", None, None),
    )
    sizes = (mesh.shape["prow"], mesh.shape["pcol"])
    return jax.shard_map(
        functools.partial(on_device, sizes),
        mesh=mesh,
        in_specs=placed,
        out_specs=P("prow", None, None, None),
        check_vma=False,
    )
```

```python
import functools

import jax
import jax.numpy as jnp
from jax import lax
from jax.experimental import pallas as pl
from jax.experimental.pallas import tpu as pltpu
from jax.sharding import PartitionSpec as P

MESH = pl.DeviceIdType.MESH
F32 = jnp.float32
BF16 = jnp.bfloat16
PIECES = 4


def kernel(dims, *refs):
    rows, cols, levels, width, half, slots = dims
    nx, ny = cols // 2, cols // 2
    nz = rows // nx
    per_col = rows // cols
    step_z = cols // nx
    (rhs_hbm, diag_hbm, low_hbm, src_hbm, tgt_hbm, out_hbm) = refs[:6]
    (rhs0, rhsh, diag, block, acc, mine, pair_out, pair_in, cross) = refs[6:15]
    low = refs[15:15 + levels - 1]
    (rhs_sem, diag_sem, low_sem, out_sem, b_send, b_recv, p_send, p_recv,
     y_send, y_recv, m_send, m_recv, src_ref, tgt_ref, table_sem) = refs[15 + levels - 1:]

    r = lax.axis_index("prow")
    c = lax.axis_index("pcol")
    z, x = r // nx, lax.rem(r, nx)
    y, core = c // 2, lax.rem(c, 2)
    other = 1 - core
    spine_x = lax.rem(c, nx)
    is_spine = x == spine_x
    first_z = c // nx
    sibling = (r, y * 2 + other)

    def across(j):
        return (r, lax.rem(y + j, ny) * 2 + core)

    loads_rhs = [pltpu.make_async_copy(rhs_hbm.at[0, 0], rhs0, rhs_sem.at[0])]
    col_half = pl.ds(pl.multiple_of(core * half, half), half)
    for l in range(1, levels):
        loads_rhs.append(pltpu.make_async_copy(
            rhs_hbm.at[0, l, :, col_half], rhsh.at[l - 1], rhs_sem.at[l]))
    loads_diag = [pltpu.make_async_copy(diag_hbm.at[0, l], diag.at[l], diag_sem.at[l])
                  for l in range(levels)]
    loads_low = [pltpu.make_async_copy(
        low_hbm.at[0, 0, l, pl.ds(0, low[l].shape[0])], low[l], low_sem.at[l])
        for l in range(levels - 1)]
    for l in range(levels):
        loads_rhs[l].start()
        loads_diag[l].start()
        if l < levels - 1:
            loads_low[l].start()

    tables = [pltpu.make_async_copy(src_hbm, src_ref, table_sem.at[0]),
              pltpu.make_async_copy(tgt_hbm, tgt_ref, table_sem.at[1])]
    for copy in tables:
        copy.start()

    barrier = pltpu.get_barrier_semaphore()

    def greet(device):
        pl.semaphore_signal(barrier, inc=1, device_id=device, device_id_type=MESH)

    greet(sibling)
    for j in range(1, ny):
        greet(across(j))

    @pl.when(is_spine)
    def _():
        for j in range(1, nx):
            greet((z * nx + lax.rem(x + j, nx), c))

        @pl.when(z > 0)
        def _():
            greet((r - nx, c))

        @pl.when(z < nz - 1)
        def _():
            greet((r + nx, c))

    @pl.when(jnp.logical_not(is_spine))
    def _():
        greet((z * nx + spine_x, c))
    ends = jnp.where(z > 0, 1, 0) + jnp.where(z < nz - 1, 1, 0)
    pl.semaphore_wait(barrier, ny + jnp.where(is_spine, nx - 1 + ends, 1))

    piece_rows = width // PIECES

    def b_copy(l, k, h, p, lane, device):
        part = block.at[l, k, h, pl.ds(p * piece_rows, piece_rows)]
        return pltpu.make_async_remote_copy(
            src_ref=part, dst_ref=part,
            send_sem=b_send.at[l, k, h, p, lane], recv_sem=b_recv.at[l, k, h, p],
            device_id=device, device_id_type=MESH)

    def on_routes(l, k, h, p, act):
        origin = first_z + k * step_z

        @pl.when(is_spine)
        def _():
            @pl.when(jnp.logical_and(z >= origin, z < nz - 1))
            def _():
                act(b_copy(l, k, h, p, 0, (r + nx, c)))

            @pl.when(jnp.logical_and(z <= origin, z > 0))
            def _():
                act(b_copy(l, k, h, p, 1, (r - nx, c)))
            for j in range(1, nx):
                act(b_copy(l, k, h, p, 1 + j, (z * nx + lax.rem(x + j, nx), c)))

    def is_root(k):
        return jnp.logical_and(is_spine, z == first_z + k * step_z)

    def publish(l, h, value):
        for k in range(per_col):
            @pl.when(is_root(k))
            def _():
                block[l, k, h] = value
                for p in range(PIECES):
                    on_routes(l, k, h, p, lambda copy: copy.start())

    def p_copy(l):
        return pltpu.make_async_remote_copy(
            src_ref=pair_out.at[l], dst_ref=pair_in.at[l], send_sem=p_send.at[l],
            recv_sem=p_recv.at[l], device_id=sibling, device_id_type=MESH)

    def y_copy(l, j):
        return pltpu.make_async_remote_copy(
            src_ref=cross.at[l, y], dst_ref=cross.at[l, y], send_sem=y_send.at[l, j - 1],
            recv_sem=y_recv.at[l, j - 1], device_id=across(j), device_id_type=MESH)

    def m_copy(l):
        return pltpu.make_async_remote_copy(
            src_ref=mine.at[l, core], dst_ref=mine.at[l, core], send_sem=m_send.at[l],
            recv_sem=m_recv.at[l], device_id=sibling, device_id_type=MESH)

    def put_out(l):
        return [pltpu.make_async_copy(
            mine.at[l, h], out_hbm.at[0, l, :, pl.ds(h * half, half)], out_sem.at[l, h])
            for h in range(2)]

    def pair_slot(l, k, t):
        slot, there = jnp.int32(0), jnp.int32(0)
        for b in range(low[l].shape[0]):
            hit = jnp.where(
                jnp.logical_and(src_ref[0, 0, l, b] == k, tgt_ref[0, 0, l, b] == t), 1, 0)
            slot, there = slot + b * hit, there + hit
        return slot, there

    def product(l, k, t, right):
        slot, there = pair_slot(l, k, t)
        value = jnp.dot(low[l][slot], right, preferred_element_type=F32)
        if per_col * (levels - 1 - l) > slots:
            value = jnp.where(there > 0, value, 0.0)
        return value

    loads_rhs[0].wait()
    loads_diag[0].wait()
    solved = jnp.dot(diag[0], rhs0[...].astype(BF16), preferred_element_type=F32).astype(BF16)
    for h in range(2):
        publish(0, h, solved[:, h * half:(h + 1) * half])
    for h in range(2):
        mine[0, h] = solved[:, h * half:(h + 1) * half]
    for copy in put_out(0):
        copy.start()

    for copy in tables:
        copy.wait()
    low_z = z < nz // 2
    for l in range(levels - 1):
        t = l + 1
        for i in range(per_col):
            k = jnp.where(low_z, i, per_col - 1 - i)
            for h in (core, other):
                @pl.when(jnp.logical_not(is_root(k)))
                def _():
                    for p in range(PIECES):
                        b_copy(l, k, h, p, 0, sibling).wait_recv()
                        on_routes(l, k, h, p, lambda copy: copy.start())
        loads_low[l].wait()

        def next_partial(h):
            total = None
            for k in range(per_col):
                value = product(l, k, t, block[l, k, h])
                total = value if total is None else total + value
            if l > 0:
                total = total + acc[t - 1, h]
            return total

        pair_out[l] = next_partial(other).astype(BF16)
        p_copy(l).start()
        own = next_partial(core)
        p_copy(l).wait_recv()
        cross[l, y] = (own + pair_in[l].astype(F32)).astype(BF16)
        for j in range(1, ny):
            y_copy(l, j).start()

        for later in range(l + 2, levels):
            total = None
            for k in range(per_col):
                right = jnp.concatenate([block[l, k, 0], block[l, k, 1]], axis=1)
                value = product(l, k, later, right)
                total = value if total is None else total + value
            for h in range(2):
                part = total[:, h * half:(h + 1) * half]
                acc[later - 1, h] = part if l == 0 else acc[later - 1, h] + part

        loads_rhs[t].wait()
        loads_diag[t].wait()
        for j in range(1, ny):
            y_copy(l, j).wait_recv()
        summed = cross[l, 0].astype(F32)
        for j in range(1, ny):
            summed = summed + cross[l, j].astype(F32)
        reduced = (rhsh[t - 1] - summed).astype(BF16)
        solved = jnp.dot(diag[t], reduced, preferred_element_type=F32).astype(BF16)
        mine[t, core] = solved
        m_copy(t).start()
        if t < levels - 1:
            publish(t, core, solved)
        m_copy(t).wait_recv()
        if t < levels - 1:
            publish(t, other, mine[t, other])
        for copy in put_out(t):
            copy.start()

    for l in range(levels):
        for copy in put_out(l):
            copy.wait()
        if l > 0:
            m_copy(l).wait_send()
        if l < levels - 1:
            p_copy(l).wait_send()
            for j in range(1, ny):
                y_copy(l, j).wait_send()
            for k in range(per_col):
                for h in range(2):
                    for p in range(PIECES):
                        on_routes(l, k, h, p, lambda copy: copy.wait_send())


def on_device(mesh_sizes, right_hand_blocks, diag_inverse, lower_blocks, block_source,
              target_level_per_slot):
    rows, cols = mesh_sizes
    _, levels, width, rhs_cols = right_hand_blocks.shape
    slots = lower_blocks.shape[3]
    half = rhs_cols // 2
    per_col = rows // cols
    nx, ny = cols // 2, cols // 2
    filled = [min(slots, per_col * (levels - 1 - l)) for l in range(levels - 1)]
    dma = pltpu.SemaphoreType.DMA
    steps = levels - 1
    piece = (width, half)
    products = sum(filled) + levels
    return pl.pallas_call(
        functools.partial(kernel, (rows, cols, levels, width, half, slots)),
        out_shape=jax.ShapeDtypeStruct((1, levels, width, rhs_cols), BF16),
        in_specs=[pl.BlockSpec(memory_space=pl.ANY)] * 5,
        out_specs=pl.BlockSpec(memory_space=pl.ANY),
        scratch_shapes=[
            pltpu.VMEM((width, rhs_cols), F32),
            pltpu.VMEM((steps,) + piece, F32),
            pltpu.VMEM((levels, width, width), BF16),
            pltpu.VMEM((steps, per_col, 2) + piece, BF16),
            pltpu.VMEM((steps, 2) + piece, F32),
            pltpu.VMEM((levels, 2) + piece, BF16),
            pltpu.VMEM((steps,) + piece, BF16),
            pltpu.VMEM((steps,) + piece, BF16),
            pltpu.VMEM((steps, ny) + piece, BF16),
        ]
        + [pltpu.VMEM((n, width, width), BF16) for n in filled]
        + [
            dma((levels,)), dma((levels,)), dma((steps,)), dma((levels, 2)),
            dma((steps, per_col, 2, PIECES, nx + 1)), dma((steps, per_col, 2, PIECES)),
            dma((steps,)), dma((steps,)),
            dma((steps, ny - 1)), dma((steps, ny - 1)),
            dma((levels,)), dma((levels,)),
            pltpu.SMEM(block_source.shape, jnp.int32),
            pltpu.SMEM(target_level_per_slot.shape, jnp.int32), dma((2,)),
        ],
        compiler_params=pltpu.CompilerParams(
            collective_id=0, has_side_effects=True, vmem_limit_bytes=56 * 2**20),
        cost_estimate=pl.CostEstimate(
            flops=2 * products * width * width * rhs_cols,
            bytes_accessed=products * width * width * 2 + levels * width * rhs_cols * 6,
            transcendentals=0),
    )(right_hand_blocks, diag_inverse, lower_blocks, block_source, target_level_per_slot)


def solution(mesh):
    placed = (
        P("prow", None, None, None),
        P("prow", None, None, None),
        P("prow", "pcol", None, None, None, None),
        P("prow", "pcol", None, None),
        P("prow", "pcol", None, None),
    )
    sizes = (mesh.shape["prow"], mesh.shape["pcol"])
    return jax.shard_map(
        functools.partial(on_device, sizes),
        mesh=mesh,
        in_specs=placed,
        out_specs=P("prow", None, None, None),
        check_vma=False,
    )
```

```python
import functools

import jax
import jax.numpy as jnp
from jax import lax
from jax.experimental import pallas as pl
from jax.experimental.pallas import tpu as pltpu
from jax.sharding import PartitionSpec as P

MESH = pl.DeviceIdType.MESH
F32 = jnp.float32
BF16 = jnp.bfloat16
PIECES = 4


def kernel(dims, *refs):
    rows, cols, levels, width, half, slots = dims
    nx, ny = cols // 2, cols // 2
    nz = rows // nx
    per_col = rows // cols
    step_z = cols // nx
    (rhs_hbm, diag_hbm, low_hbm, src_hbm, tgt_hbm, out_hbm) = refs[:6]
    (rhs0, rhsh, diag, block, acc, mine, pair_out, pair_in, cross) = refs[6:15]
    low = refs[15:15 + levels - 1]
    (rhs_sem, diag_sem, low_sem, out_sem, b_send, b_recv, p_send, p_recv,
     y_send, y_recv, m_send, m_recv, src_ref, tgt_ref, table_sem) = refs[15 + levels - 1:]

    r = lax.axis_index("prow")
    c = lax.axis_index("pcol")
    z, x = r // nx, lax.rem(r, nx)
    y, core = c // 2, lax.rem(c, 2)
    other = 1 - core
    spine_x = lax.rem(c, nx)
    is_spine = x == spine_x
    first_z = c // nx
    sibling = (r, y * 2 + other)

    def across(j):
        return (r, lax.rem(y + j, ny) * 2 + core)

    loads_rhs = [pltpu.make_async_copy(rhs_hbm.at[0, 0], rhs0, rhs_sem.at[0])]
    col_half = pl.ds(pl.multiple_of(core * half, half), half)
    for l in range(1, levels):
        loads_rhs.append(pltpu.make_async_copy(
            rhs_hbm.at[0, l, :, col_half], rhsh.at[l - 1], rhs_sem.at[l]))
    loads_diag = [pltpu.make_async_copy(diag_hbm.at[0, l], diag.at[l], diag_sem.at[l])
                  for l in range(levels)]
    loads_low = [pltpu.make_async_copy(
        low_hbm.at[0, 0, l, pl.ds(0, low[l].shape[0])], low[l], low_sem.at[l])
        for l in range(levels - 1)]
    for l in range(levels):
        loads_rhs[l].start()
        loads_diag[l].start()
        if l < levels - 1:
            loads_low[l].start()

    tables = [pltpu.make_async_copy(src_hbm, src_ref, table_sem.at[0]),
              pltpu.make_async_copy(tgt_hbm, tgt_ref, table_sem.at[1])]
    for copy in tables:
        copy.start()

    barrier = pltpu.get_barrier_semaphore()

    def greet(device):
        pl.semaphore_signal(barrier, inc=1, device_id=device, device_id_type=MESH)

    greet(sibling)
    for j in range(1, ny):
        greet(across(j))

    @pl.when(is_spine)
    def _():
        for j in range(1, nx):
            greet((z * nx + lax.rem(x + j, nx), c))

        @pl.when(z > 0)
        def _():
            greet((r - nx, c))

        @pl.when(z < nz - 1)
        def _():
            greet((r + nx, c))

    @pl.when(jnp.logical_not(is_spine))
    def _():
        greet((z * nx + spine_x, c))
    ends = jnp.where(z > 0, 1, 0) + jnp.where(z < nz - 1, 1, 0)

    piece_rows = width // PIECES

    def b_copy(l, k, h, p, lane, device):
        part = block.at[l, k, h, pl.ds(p * piece_rows, piece_rows)]
        return pltpu.make_async_remote_copy(
            src_ref=part, dst_ref=part,
            send_sem=b_send.at[l, k, h, p, lane], recv_sem=b_recv.at[l, k, h, p],
            device_id=device, device_id_type=MESH)

    def on_routes(l, k, h, p, act):
        origin = first_z + k * step_z

        @pl.when(is_spine)
        def _():
            @pl.when(jnp.logical_and(z >= origin, z < nz - 1))
            def _():
                act(b_copy(l, k, h, p, 0, (r + nx, c)))

            @pl.when(jnp.logical_and(z <= origin, z > 0))
            def _():
                act(b_copy(l, k, h, p, 1, (r - nx, c)))
            for j in range(1, nx):
                act(b_copy(l, k, h, p, 1 + j, (z * nx + lax.rem(x + j, nx), c)))

    def is_root(k):
        return jnp.logical_and(is_spine, z == first_z + k * step_z)

    def publish(l, h, value):
        for k in range(per_col):
            @pl.when(is_root(k))
            def _():
                block[l, k, h] = value
                for p in range(PIECES):
                    on_routes(l, k, h, p, lambda copy: copy.start())

    def p_copy(l):
        return pltpu.make_async_remote_copy(
            src_ref=pair_out.at[l], dst_ref=pair_in.at[l], send_sem=p_send.at[l],
            recv_sem=p_recv.at[l], device_id=sibling, device_id_type=MESH)

    def y_copy(l, j):
        return pltpu.make_async_remote_copy(
            src_ref=cross.at[l, y], dst_ref=cross.at[l, y], send_sem=y_send.at[l, j - 1],
            recv_sem=y_recv.at[l, j - 1], device_id=across(j), device_id_type=MESH)

    def m_copy(l):
        return pltpu.make_async_remote_copy(
            src_ref=mine.at[l, core], dst_ref=mine.at[l, core], send_sem=m_send.at[l],
            recv_sem=m_recv.at[l], device_id=sibling, device_id_type=MESH)

    def put_out(l):
        return [pltpu.make_async_copy(
            mine.at[l, h], out_hbm.at[0, l, :, pl.ds(h * half, half)], out_sem.at[l, h])
            for h in range(2)]

    def pair_slot(l, k, t):
        slot, there = jnp.int32(0), jnp.int32(0)
        for b in range(low[l].shape[0]):
            hit = jnp.where(
                jnp.logical_and(src_ref[0, 0, l, b] == k, tgt_ref[0, 0, l, b] == t), 1, 0)
            slot, there = slot + b * hit, there + hit
        return slot, there

    def product(l, k, t, right):
        slot, there = pair_slot(l, k, t)
        value = jnp.dot(low[l][slot], right, preferred_element_type=F32)
        if per_col * (levels - 1 - l) > slots:
            value = jnp.where(there > 0, value, 0.0)
        return value

    loads_rhs[0].wait()
    loads_diag[0].wait()
    solved = jnp.dot(diag[0], rhs0[...].astype(BF16), preferred_element_type=F32).astype(BF16)
    pl.semaphore_wait(barrier, ny + jnp.where(is_spine, nx - 1 + ends, 1))
    for h in range(2):
        publish(0, h, solved[:, h * half:(h + 1) * half])
    for h in range(2):
        mine[0, h] = solved[:, h * half:(h + 1) * half]
    for copy in put_out(0):
        copy.start()

    for copy in tables:
        copy.wait()
    low_z = z < nz // 2
    for l in range(levels - 1):
        t = l + 1
        for i in range(per_col):
            k = jnp.where(low_z, i, per_col - 1 - i)
            for h in (core, other):
                @pl.when(jnp.logical_not(is_root(k)))
                def _():
                    for p in range(PIECES):
                        b_copy(l, k, h, p, 0, sibling).wait_recv()
                        on_routes(l, k, h, p, lambda copy: copy.start())
        loads_low[l].wait()

        def next_partial(h):
            total = None
            for k in range(per_col):
                value = product(l, k, t, block[l, k, h])
                total = value if total is None else total + value
            if l > 0:
                total = total + acc[t - 1, h]
            return total

        pair_out[l] = next_partial(other).astype(BF16)
        p_copy(l).start()
        own = next_partial(core)
        p_copy(l).wait_recv()
        cross[l, y] = (own + pair_in[l].astype(F32)).astype(BF16)
        for j in range(1, ny):
            y_copy(l, j).start()

        for later in range(l + 2, levels):
            total = None
            for k in range(per_col):
                right = jnp.concatenate([block[l, k, 0], block[l, k, 1]], axis=1)
                value = product(l, k, later, right)
                total = value if total is None else total + value
            for h in range(2):
                part = total[:, h * half:(h + 1) * half]
                acc[later - 1, h] = part if l == 0 else acc[later - 1, h] + part

        loads_rhs[t].wait()
        loads_diag[t].wait()
        for j in range(1, ny):
            y_copy(l, j).wait_recv()
        summed = cross[l, 0].astype(F32)
        for j in range(1, ny):
            summed = summed + cross[l, j].astype(F32)
        reduced = (rhsh[t - 1] - summed).astype(BF16)
        solved = jnp.dot(diag[t], reduced, preferred_element_type=F32).astype(BF16)
        mine[t, core] = solved
        m_copy(t).start()
        if t < levels - 1:
            publish(t, core, solved)
        m_copy(t).wait_recv()
        if t < levels - 1:
            publish(t, other, mine[t, other])
        for copy in put_out(t):
            copy.start()

    for l in range(levels):
        for copy in put_out(l):
            copy.wait()
        if l > 0:
            m_copy(l).wait_send()
        if l < levels - 1:
            p_copy(l).wait_send()
            for j in range(1, ny):
                y_copy(l, j).wait_send()
            for k in range(per_col):
                for h in range(2):
                    for p in range(PIECES):
                        on_routes(l, k, h, p, lambda copy: copy.wait_send())


def on_device(mesh_sizes, right_hand_blocks, diag_inverse, lower_blocks, block_source,
              target_level_per_slot):
    rows, cols = mesh_sizes
    _, levels, width, rhs_cols = right_hand_blocks.shape
    slots = lower_blocks.shape[3]
    half = rhs_cols // 2
    per_col = rows // cols
    nx, ny = cols // 2, cols // 2
    filled = [min(slots, per_col * (levels - 1 - l)) for l in range(levels - 1)]
    dma = pltpu.SemaphoreType.DMA
    steps = levels - 1
    piece = (width, half)
    products = sum(filled) + levels
    return pl.pallas_call(
        functools.partial(kernel, (rows, cols, levels, width, half, slots)),
        out_shape=jax.ShapeDtypeStruct((1, levels, width, rhs_cols), BF16),
        in_specs=[pl.BlockSpec(memory_space=pl.ANY)] * 5,
        out_specs=pl.BlockSpec(memory_space=pl.ANY),
        scratch_shapes=[
            pltpu.VMEM((width, rhs_cols), F32),
            pltpu.VMEM((steps,) + piece, F32),
            pltpu.VMEM((levels, width, width), BF16),
            pltpu.VMEM((steps, per_col, 2) + piece, BF16),
            pltpu.VMEM((steps, 2) + piece, F32),
            pltpu.VMEM((levels, 2) + piece, BF16),
            pltpu.VMEM((steps,) + piece, BF16),
            pltpu.VMEM((steps,) + piece, BF16),
            pltpu.VMEM((steps, ny) + piece, BF16),
        ]
        + [pltpu.VMEM((n, width, width), BF16) for n in filled]
        + [
            dma((levels,)), dma((levels,)), dma((steps,)), dma((levels, 2)),
            dma((steps, per_col, 2, PIECES, nx + 1)), dma((steps, per_col, 2, PIECES)),
            dma((steps,)), dma((steps,)),
            dma((steps, ny - 1)), dma((steps, ny - 1)),
            dma((levels,)), dma((levels,)),
            pltpu.SMEM(block_source.shape, jnp.int32),
            pltpu.SMEM(target_level_per_slot.shape, jnp.int32), dma((2,)),
        ],
        compiler_params=pltpu.CompilerParams(
            collective_id=0, has_side_effects=True, vmem_limit_bytes=56 * 2**20),
        cost_estimate=pl.CostEstimate(
            flops=2 * products * width * width * rhs_cols,
            bytes_accessed=products * width * width * 2 + levels * width * rhs_cols * 6,
            transcendentals=0),
    )(right_hand_blocks, diag_inverse, lower_blocks, block_source, target_level_per_slot)


def solution(mesh):
    placed = (
        P("prow", None, None, None),
        P("prow", None, None, None),
        P("prow", "pcol", None, None, None, None),
        P("prow", "pcol", None, None),
        P("prow", "pcol", None, None),
    )
    sizes = (mesh.shape["prow"], mesh.shape["pcol"])
    return jax.shard_map(
        functools.partial(on_device, sizes),
        mesh=mesh,
        in_specs=placed,
        out_specs=P("prow", None, None, None),
        check_vma=False,
    )
```
